32 devices in a mesh: grp: 2 (over x), slab: 8 (over z, y), blk: 2 (over core).
Axes of the slice: x: 2, y: 2, z: 4, core: 2. Of those that a mesh axis runs over, the one named last changes fastest.
Arguments:
- volume: float32 [256, 8192], P(('grp', 'slab'), 'blk'), parts along dimension 0, may hold values from -6 to 6
- measured: float32 [6, 2048, 3072], P('grp', 'slab', 'blk'), parts along dimension 0, may hold values from -6 to 6
- band_start: int32 [3, 8], replicated, may hold values from 0 to 1536, as said below
- band_length: int32 [3, 8], replicated, may hold values from 257 to 512, as said below
- row_offset: int32 [3, 2, 128], replicated, may hold values from 0 to 511, as said below
- row_weight: float32 [3, 2, 128], replicated, may hold values from 0.2 to 1
- col_index: int32 [3, 2, 8192], replicated, may hold values from 0 to 3071, as said below
- col_weight: float32 [3, 2, 8192], replicated, may hold values from 0.2 to 1
Outputs:
- residual: float32 [6, 2048, 3072], P('grp', 'slab', 'blk'), parts along dimension 0
- gradient: float32 [256, 8192], P(('grp', 'slab'), 'blk'), parts along dimension 0
The draws below stay inside these ranges and needn't reach their ends.
There are 2 independent parts, one for each index of `grp`. The reference program is written for one: setup_inputs(seed, part) draws one part's arguments, and reference() takes and returns one part's arrays. A program takes and returns all parts, laid end to end along the dimension named above; an argument that names none is the same for every part. Nothing has to cross between parts.
Inputs may be any that keep to these rules, and one draw needn't show every extreme that they name: Slab s's band in a view starts between (s - 1) * 256 and s * 256, and ends inside the panel: band_start + 512 <= 2048. `band_length`: at most 512, which some slab reaches in every view. `row_offset`: the taps of a slice are consecutive rows. `col_index`: the taps of a voxel column are consecutive columns.
All inputs are finite; a program needn't handle non-finite values.
Results may differ from the reference program's by a relative error of at most 0.0001.
Values sent between devices are 32-bit elements; how exact they have to be, the bound alone decides.
A program may use at most 128 MiB of HBM per device.

```python
import jax
import jax.numpy as jnp

U = 3072
R = 2048
VIEWS = 3
TAPS = 2
ZS = 16
NZ = 128
NXY = 8192
RO = 256
BAND = 512


def band_lengths(key):
    key = jax.random.fold_in(key, 11)
    len_key, long_key = jax.random.split(key)
    slab_count = NZ // ZS
    base_len = jax.random.randint(len_key, (VIEWS, slab_count), RO + 1, BAND + 1)
    longest = jax.random.randint(long_key, (VIEWS, 1), 0, slab_count)
    slab_ids = jnp.arange(slab_count)[None, :]
    return jnp.where(slab_ids == longest, BAND, base_len).astype(jnp.int32)


def draw_band_length(key, part):
    return band_lengths(key)


def draw_row_offset(key, part):
    key = jax.random.fold_in(key, 3)
    in_slab = (jnp.arange(NZ) % ZS)[None, :]
    jitter = jax.random.randint(key, (VIEWS, NZ), 0, 2)
    jitter = jnp.where((in_slab == 0) | (in_slab == ZS - 1), 0, jitter)
    first_tap = jnp.minimum(in_slab * (BAND - TAPS) // (ZS - 1) + jitter, BAND - TAPS)
    taps_ids = jnp.arange(TAPS)[None, :, None]
    return (first_tap[:, None, :] + taps_ids).astype(jnp.int32)


def draw_band_start(key, part):
    key = jax.random.fold_in(key, 5)
    slab_count = NZ // ZS
    backoff = jax.random.randint(key, (VIEWS, slab_count), 0, RO + 1)
    slab_ids = jnp.arange(slab_count)[None, :]
    return jnp.clip(slab_ids * RO - backoff, 0, R - BAND).astype(jnp.int32)


def draw_col_index(key, part):
    key = jax.random.fold_in(key, 7)
    first_col = jax.random.randint(key, (VIEWS, 1, NXY), 0, U - TAPS + 1)
    taps_ids = jnp.arange(TAPS)[None, :, None]
    return (first_col + taps_ids).astype(jnp.int32)


def steps_of(stream_key, dims, cuts, smallest, high):
    level = 1.0
    for position, shards_of in cuts:
        heights = jax.random.uniform(jax.random.fold_in(jax.random.fold_in(stream_key, 6), position), (shards_of,), jnp.float32, smallest / len(cuts), high / len(cuts))
        level = level * jnp.repeat(jnp.exp(heights), dims[position] // shards_of).reshape((-1,) + (1,) * (len(dims) - 1 - position))
    return level


def noise(own_key, shape, deviation, bound, pieces=(), kind=jnp.bfloat16):
    drawn = jax.random.normal(own_key, shape, jnp.float32) * deviation
    if len(pieces) > 0:
        drawn = steps_of(own_key, shape, pieces, -0.22, 0.18) * drawn
    return jnp.clip(drawn, min=-bound, max=bound).astype(kind)


def setup_inputs(seed: int = 0, part: int = 0) -> dict:
    arg_keys = jax.random.split(jax.random.key(seed), 9)
    part_keys = jax.random.split(jax.random.fold_in(arg_keys[8], part), 9)
    volume = noise(part_keys[0], (NZ, NXY), 1.0, 6.0, ((0, 8), (1, 2)), jnp.float32)
    measured = noise(part_keys[1], (VIEWS, R, U), 1.0, 6.0, ((1, 8), (2, 2)), jnp.float32)
    band_start = draw_band_start(jax.random.fold_in(arg_keys[8], 71), part)
    band_length = draw_band_length(jax.random.fold_in(arg_keys[8], 71), part)
    row_offset = draw_row_offset(jax.random.fold_in(arg_keys[8], 71), part)
    row_weight = jnp.clip(jax.random.uniform(arg_keys[5], (VIEWS, TAPS, NZ), jnp.float32, 0.2, 1.0), 0.2, 1.0)
    col_index = draw_col_index(jax.random.fold_in(arg_keys[8], 71), part)
    col_weight = jnp.clip(jax.random.uniform(arg_keys[7], (VIEWS, TAPS, NXY), jnp.float32, 0.2, 1.0), 0.2, 1.0)
    return {"volume": volume, "measured": measured, "band_start": band_start, "band_length": band_length, "row_offset": row_offset, "row_weight": row_weight, "col_index": col_index, "col_weight": col_weight}


def reference(volume, measured, band_start, band_length, row_offset, row_weight, col_index, col_weight):
    nz_cells, xy_cells = volume.shape
    view_count, panel_rows, panel_cols = measured.shape
    slab_of = (jnp.arange(nz_cells) // ZS).astype(jnp.int32)
    residuals = []
    gradient = jnp.zeros((nz_cells, xy_cells), jnp.float32)
    for view_id in range(view_count):
        values = volume[:, None, :] * col_weight[view_id][None, :, :]
        spread = jnp.zeros((nz_cells, panel_cols), jnp.float32).at[:, col_index[view_id].reshape(-1)].add(values.reshape(nz_cells, -1))
        absolute = band_start[view_id][slab_of][None, :] + row_offset[view_id]
        contrib = row_weight[view_id][:, :, None] * spread[None, :, :]
        projection = jnp.zeros((panel_rows, panel_cols), jnp.float32).at[absolute.reshape(-1)].add(contrib.reshape(-1, panel_cols))
        residual = measured[view_id] - projection
        inside = row_offset[view_id] < band_length[view_id][slab_of][None, :]
        picked = jnp.where(inside[:, :, None], residual[absolute], 0.0)
        along_rows = jnp.sum(row_weight[view_id][:, :, None] * picked, axis=0)
        gradient = gradient + jnp.sum(along_rows[:, col_index[view_id]] * col_weight[view_id][None, :, :], axis=1)
        residuals.append(residual)
    return jnp.stack(residuals), gradient / VIEWS
```

```python
import jax
import jax.numpy as jnp
from jax import lax
from jax.experimental import pallas as pl
from jax.experimental.pallas import tpu as pltpu
from jax.sharding import PartitionSpec as P

HIGH = lax.Precision.HIGHEST
F32 = jnp.float32
BF16 = jnp.bfloat16
LOW = 256
CHUNK = 1024
SLOT = 64


def split(x):
    high = x.astype(BF16)
    return high, (x - high.astype(F32)).astype(BF16)


def dot(a, b):
    return jnp.dot(a, b, preferred_element_type=F32)


def kernel(
    volume, col_index, col_weight, lanes, columns, measured, residual, gradient,
    low_hot, panel, frame, spread, from_core, mine, from_slabs, stack, wide, along,
    along_in, along_sum, along_core, taps_left, core_send, core_recv, slab_send, slab_recv,
    back_send, back_recv, last_send, last_recv, read_sem, write_sem,
):
    slab, blk = lax.axis_index("slab"), lax.axis_index("blk")
    slabs = lax.axis_size("slab")
    other = 1 - blk
    depth, cells = volume.shape
    views, rows, part = measured.shape
    groups = 2 * part // LOW
    chunks = cells // CHUNK
    has_lower, has_upper = slab > 0, slab < slabs - 1

    reads = [
        pltpu.make_async_copy(measured.at[v], frame.at[v], read_sem.at[v]) for v in range(views)
    ]
    for copy in reads:
        copy.start()
    barrier = pltpu.get_barrier_semaphore()
    pl.semaphore_signal(barrier, inc=1, device_id={"blk": other})

    @pl.when(has_lower)
    def _():
        pl.semaphore_signal(barrier, inc=1, device_id={"slab": slab - 1})

    @pl.when(has_upper)
    def _():
        pl.semaphore_signal(barrier, inc=1, device_id={"slab": slab + 1})

    pl.semaphore_wait(barrier, 1 + jnp.where(has_lower, 1, 0) + jnp.where(has_upper, 1, 0))

    def remote(source, target, send, recv, device):
        return pltpu.make_async_remote_copy(
            src_ref=source, dst_ref=target, send_sem=send, recv_sem=recv, device_id=device
        )

    def voxel_rows(v, j):
        at = pl.ds(pl.multiple_of(blk * cells + j * CHUNK, CHUNK), CHUNK)
        index, weight = col_index[v, :, at], col_weight[v, :, at]
        first, second = index[0:1], index[1:2]
        ordered = first <= second
        base = jnp.minimum(first, second)
        wa = jnp.where(ordered, weight[0:1], weight[1:2])
        wb = jnp.where(ordered, weight[1:2], weight[0:1])
        return lax.shift_right_logical(base, 8), lax.bitwise_and(base, LOW - 1), wa, wb

    my_cols = pl.ds(pl.multiple_of(blk * part, 128), part)
    other_cols = pl.ds(pl.multiple_of(other * part, 128), part)

    def core_copy(v):
        return remote(
            spread.at[v, :, other_cols], from_core.at[v], core_send.at[v], core_recv.at[v],
            {"blk": other},
        )

    def slab_copy(v, way):
        return remote(
            mine.at[v], from_slabs.at[v, 1 - way], slab_send.at[v, way],
            slab_recv.at[v, 1 - way], {"slab": slab + (2 * way - 1)},
        )

    def back_copy(v, way):
        return remote(
            along.at[v, pl.ds(2 * depth * way, depth)], along_in.at[v, 1 - way],
            back_send.at[v, way], back_recv.at[v, 1 - way], {"slab": slab + (2 * way - 1)},
        )

    def last_copy(v):
        return remote(
            along_sum.at[v], along_core.at[v], last_send.at[v], last_recv.at[v], {"blk": other}
        )

    def start_both(make, v):
        @pl.when(has_lower)
        def _():
            make(v, 0).start()

        @pl.when(has_upper)
        def _():
            make(v, 1).start()

    def await_both(make, v):
        @pl.when(has_lower)
        def _():
            make(v, 1).wait_recv()

        @pl.when(has_upper)
        def _():
            make(v, 0).wait_recv()

    def await_sent(make, v):
        @pl.when(has_lower)
        def _():
            make(v, 0).wait_send()

        @pl.when(has_upper)
        def _():
            make(v, 1).wait_send()

    @pl.when(slab == 0)
    def _():
        from_slabs[:, 0] = jnp.zeros((views, depth, part), F32)
        along_in[:, 0] = jnp.zeros((views, depth, part), F32)

    @pl.when(slab == slabs - 1)
    def _():
        from_slabs[:, 1] = jnp.zeros((views, depth, part), F32)
        along_in[:, 1] = jnp.zeros((views, depth, part), F32)

    def spread_view(v):
        panel[...] = jnp.zeros_like(panel)

        def step(j, carry):
            at = pl.ds(pl.multiple_of(j * CHUNK, CHUNK), CHUNK)
            high, low, wa, wb = voxel_rows(v, j)
            ids = lax.broadcasted_iota(jnp.int32, (LOW, CHUNK), 0)
            hot = jnp.where(ids == low, 1.0, 0.0).astype(BF16)
            low_hot[v, :, at] = hot
            values = volume[:, at]
            pieces = split(values * wa) + split(values * wb)
            high = jnp.broadcast_to(high, (depth, CHUNK))
            parts = []
            for h in range(groups):
                here = jnp.where(high == h, 1.0, 0.0).astype(BF16)
                parts += [piece * here for piece in pieces]
            panel[...] += lax.dot_general(
                jnp.concatenate(parts, axis=0), hot, (((1,), (1,)), ((), ())),
                preferred_element_type=F32,
            )
            return carry

        lax.fori_loop(0, chunks, step, 0)
        for h in range(groups):
            own = panel[4 * depth * h : 4 * depth * (h + 1)]
            at = slice(LOW * h, LOW * (h + 1))
            spread[v, :, at] = own[0:depth] + own[depth : 2 * depth]
            wide[:, at] = own[2 * depth : 3 * depth] + own[3 * depth :]
        spread[v] = spread[v] + pltpu.roll(wide[...], 1, 1)

    def pass_on(v):
        core_copy(v).wait_recv()
        mine[v] = spread[v, :, my_cols] + from_core[v]
        start_both(slab_copy, v)

    for v in range(views):
        spread_view(v)
        core_copy(v).start()
        if v > 0:
            pass_on(v - 1)

    def row_matrices(v):
        ids = lax.broadcasted_iota(jnp.int32, (rows, 4 * SLOT), 0).astype(F32)
        p = lanes[v]
        project = jnp.where(ids == p[0:1], p[2:3], 0.0) + jnp.where(ids == p[1:2], p[3:4], 0.0)
        ids = lax.broadcasted_iota(jnp.int32, (SLOT, rows), 1).astype(F32)
        p = columns[v]
        back = jnp.where(ids == p[:, 0:1], p[:, 4:5], 0.0)
        back = back + jnp.where(ids == p[:, 1:2], p[:, 5:6], 0.0)
        return project, back

    def by_slot(x):
        high, low = split(x)
        slot = lax.broadcasted_iota(jnp.int32, x.shape, 1) < 2 * SLOT
        return jnp.where(slot, high.astype(F32), low.astype(F32)).astype(BF16)

    mixes, projects = [], []
    for v in range(views):
        if v == 1:
            pass_on(views - 1)
        project, back = row_matrices(v)
        mixes.append(
            by_slot(jnp.dot(back, project, precision=HIGH, preferred_element_type=F32))
        )
        projects.append(by_slot(project))
        back_high, back_low = split(back)
        reads[v].wait()
        data_high, data_low = split(frame[v])
        both = dot(jnp.concatenate([back_high, back_low], axis=0), data_high)
        along[v] = both[:SLOT] + both[SLOT:] + dot(back_high, data_low)

    for v in range(views):
        await_both(slab_copy, v)
        slices = jnp.concatenate(
            [from_slabs[v, 0], mine[v], from_slabs[v, 1], jnp.zeros((SLOT - 3 * depth, part), F32)],
            axis=0,
        )
        high, low = split(slices)
        stack[v, 0:SLOT] = high
        stack[v, SLOT : 2 * SLOT] = low
        stack[v, 2 * SLOT : 3 * SLOT] = high
        stack[v, 3 * SLOT :] = low
        along[v] = along[v] - dot(mixes[v], stack[v])
        start_both(back_copy, v)

    writes = [
        pltpu.make_async_copy(frame.at[v], residual.at[v], write_sem.at[v]) for v in range(views)
    ]

    def collect(v):
        await_both(back_copy, v)
        along_sum[v] = along[v, depth : 2 * depth] + along_in[v, 0] + along_in[v, 1]
        last_copy(v).start()

    for v in range(views):
        frame[v] = frame[v] - dot(projects[v], stack[v])
        writes[v].start()
        collect(v)

    gradient[...] = jnp.zeros_like(gradient)
    for v in range(views):
        last_copy(v).wait_recv()
        wide[:, my_cols] = along_sum[v]
        wide[:, other_cols] = along_core[v]
        here = wide[...]
        for t, values in enumerate((here, pltpu.roll(here, 2 * part - 1, 1))):
            for piece, x in enumerate(split(values)):
                for h in range(groups):
                    taps_left[piece, t, depth * h : depth * (h + 1)] = x[:, LOW * h : LOW * (h + 1)]

        def step(j, carry):
            at = pl.ds(pl.multiple_of(j * CHUNK, CHUNK), CHUNK)
            high, _, wa, wb = voxel_rows(v, j)
            high = jnp.broadcast_to(high, (depth, CHUNK))
            hot = low_hot[v, :, at]
            total = gradient[:, at]
            for t, w in enumerate((wa, wb)):
                picked = dot(taps_left[0, t], hot) + dot(taps_left[1, t], hot)
                found = picked[:depth]
                for h in range(1, groups):
                    found = jnp.where(high == h, picked[depth * h : depth * (h + 1)], found)
                total = total + found * w
            gradient[:, at] = total
            return carry

        lax.fori_loop(0, chunks, step, 0)
    gradient[...] = gradient[...] * (1.0 / views)

    for v in range(views):
        core_copy(v).wait_send()
        await_sent(slab_copy, v)
        await_sent(back_copy, v)
        last_copy(v).wait_send()
        writes[v].wait()


def on_device(
    volume, measured, band_start, band_length, row_offset, row_weight, col_index, col_weight
):
    slab = lax.axis_index("slab")
    depth, cells = volume.shape
    views, rows, part = measured.shape
    taps = row_offset.shape[1]
    start = jnp.repeat(band_start, depth, axis=1)[:, None, :]
    length = jnp.repeat(band_length, depth, axis=1)[:, None, :]
    row = (start + row_offset - slab * rows).astype(F32)
    live = jnp.where(row_offset < length, row_weight, 0.0)
    rest = jnp.zeros((views, 8 - 3 * taps, row.shape[2]), F32)
    table = jnp.concatenate([row, row_weight, live, rest], axis=1)
    table = jnp.pad(table, ((0, 0), (0, 0), (depth, depth)))
    table = lax.dynamic_slice_in_dim(table, slab * depth, 3 * depth, 2)
    table = jnp.pad(table, ((0, 0), (0, 0), (0, SLOT - 3 * depth)))
    lanes = jnp.tile(table, (1, 1, 4))
    columns = jnp.swapaxes(table, 1, 2)

    vmem, dma = pltpu.VMEM, pltpu.SemaphoreType.DMA
    in_vmem, anywhere = pl.BlockSpec(memory_space=pltpu.VMEM), pl.BlockSpec(memory_space=pl.ANY)
    groups = 2 * part // LOW
    return pl.pallas_call(
        kernel,
        out_shape=(
            jax.ShapeDtypeStruct(measured.shape, F32),
            jax.ShapeDtypeStruct(volume.shape, F32),
        ),
        in_specs=[in_vmem] * 5 + [anywhere],
        out_specs=(anywhere, in_vmem),
        scratch_shapes=[
            vmem((views, LOW, cells), BF16),
            vmem((4 * depth * groups, LOW), F32),
            vmem((views, rows, part), F32),
            vmem((views, depth, 2 * part), F32),
            vmem((views, depth, part), F32),
            vmem((views, depth, part), F32),
            vmem((views, 2, depth, part), F32),
            vmem((views, 4 * SLOT, part), BF16),
            vmem((depth, 2 * part), F32),
            vmem((views, SLOT, part), F32),
            vmem((views, 2, depth, part), F32),
            vmem((views, depth, part), F32),
            vmem((views, depth, part), F32),
            vmem((2, 2, depth * groups, LOW), BF16),
            dma((views,)),
            dma((views,)),
            dma((views, 2)),
            dma((views, 2)),
            dma((views, 2)),
            dma((views, 2)),
            dma((views,)),
            dma((views,)),
            dma((views,)),
            dma((views,)),
        ],
        compiler_params=pltpu.CompilerParams(
            collective_id=0, has_side_effects=True, vmem_limit_bytes=56 * 1024 * 1024
        ),
    )(volume, col_index, col_weight, lanes, columns, measured)


def solution(mesh):
    return jax.shard_map(
        on_device,
        mesh=mesh,
        in_specs=(P(("grp", "slab"), "blk"), P("grp", "slab", "blk"), P(), P(), P(), P(), P(), P()),
        out_specs=(P("grp", "slab", "blk"), P(("grp", "slab"), "blk")),
        check_vma=False,
    )
```

```python
import jax
import jax.numpy as jnp
from jax import lax
from jax.experimental import pallas as pl
from jax.experimental.pallas import tpu as pltpu
from jax.sharding import PartitionSpec as P

HIGH = lax.Precision.HIGHEST
F32 = jnp.float32
BF16 = jnp.bfloat16
LOW = 256
CHUNK = 1024
SLOT = 64


def split(x):
    high = x.astype(BF16)
    return high, (x - high.astype(F32)).astype(BF16)


def dot(a, b):
    return jnp.dot(a, b, preferred_element_type=F32)


def order_of(views):
    turns = [(step + 2 * view, -view, step, view) for view in range(views) for step in range(9)]
    return [(step, view) for _, _, step, view in sorted(turns)]


def kernel(
    volume, col_index, col_weight, lanes, columns, measured, residual, gradient,
    low_hot, panel, frame, spread, from_core, mine, from_pair, from_far, stack, wide, along,
    far_in, pair_out, pair_in, along_sum, along_core, taps_left, core_send, core_recv,
    pair_send, pair_recv, pass_send, pass_recv, far_send, far_recv, near_send, near_recv,
    last_send, last_recv, read_sem, write_sem,
):
    slab, blk = lax.axis_index("slab"), lax.axis_index("blk")
    slabs = lax.axis_size("slab")
    other = 1 - blk
    depth, cells = volume.shape
    views, rows, part = measured.shape
    groups = 2 * part // LOW
    chunks = cells // CHUNK
    pair = slab + 1 - 2 * lax.rem(slab, 2)
    onward, backward = slab + 2 * (pair - slab), slab - 2 * (pair - slab)
    has_onward = jnp.logical_and(onward >= 0, onward < slabs)
    has_backward = jnp.logical_and(backward >= 0, backward < slabs)

    reads = [
        pltpu.make_async_copy(measured.at[v], frame.at[v], read_sem.at[v]) for v in range(views)
    ]
    for copy in reads:
        copy.start()
    barrier = pltpu.get_barrier_semaphore()
    pl.semaphore_signal(barrier, inc=1, device_id={"blk": other})

    pl.semaphore_signal(barrier, inc=1, device_id={"slab": pair})

    @pl.when(has_onward)
    def _():
        pl.semaphore_signal(barrier, inc=1, device_id={"slab": onward})

    @pl.when(has_backward)
    def _():
        pl.semaphore_signal(barrier, inc=1, device_id={"slab": backward})

    pl.semaphore_wait(barrier, 2 + jnp.where(has_onward, 1, 0) + jnp.where(has_backward, 1, 0))

    def remote(source, target, send, recv, device):
        return pltpu.make_async_remote_copy(
            src_ref=source, dst_ref=target, send_sem=send, recv_sem=recv, device_id=device
        )

    def voxel_rows(v, j):
        at = pl.ds(pl.multiple_of(blk * cells + j * CHUNK, CHUNK), CHUNK)
        index, weight = col_index[v, :, at], col_weight[v, :, at]
        first, second = index[0:1], index[1:2]
        ordered = first <= second
        base = jnp.minimum(first, second)
        wa = jnp.where(ordered, weight[0:1], weight[1:2])
        wb = jnp.where(ordered, weight[1:2], weight[0:1])
        return lax.shift_right_logical(base, 8), lax.bitwise_and(base, LOW - 1), wa, wb

    my_cols = pl.ds(pl.multiple_of(blk * part, 128), part)
    other_cols = pl.ds(pl.multiple_of(other * part, 128), part)

    def core_copy(v):
        return remote(
            spread.at[v, :, other_cols], from_core.at[v], core_send.at[v], core_recv.at[v],
            {"blk": other},
        )

    def pair_copy(v):
        return remote(
            mine.at[v], from_pair.at[v], pair_send.at[v], pair_recv.at[v], {"slab": pair}
        )

    def pass_copy(v):
        return remote(
            from_pair.at[v], from_far.at[v], pass_send.at[v], pass_recv.at[v], {"slab": onward}
        )

    def far_copy(v):
        return remote(
            along.at[v, pl.ds(2 * depth, depth)], far_in.at[v], far_send.at[v], far_recv.at[v],
            {"slab": backward},
        )

    def near_copy(v):
        return remote(
            pair_out.at[v], pair_in.at[v], near_send.at[v], near_recv.at[v], {"slab": pair}
        )

    def last_copy(v):
        return remote(
            along_sum.at[v], along_core.at[v], last_send.at[v], last_recv.at[v], {"blk": other}
        )

    @pl.when(jnp.logical_not(has_backward))
    def _():
        from_far[...] = jnp.zeros_like(from_far)

    @pl.when(jnp.logical_not(has_onward))
    def _():
        far_in[...] = jnp.zeros_like(far_in)

    def spread_view(v):
        panel[...] = jnp.zeros_like(panel)

        def step(j, carry):
            at = pl.ds(pl.multiple_of(j * CHUNK, CHUNK), CHUNK)
            high, low, wa, wb = voxel_rows(v, j)
            ids = lax.broadcasted_iota(jnp.int32, (LOW, CHUNK), 0)
            hot = jnp.where(ids == low, 1.0, 0.0).astype(BF16)
            low_hot[v, :, at] = hot
            values = volume[:, at]
            pieces = split(values * wa) + split(values * wb)
            high = jnp.broadcast_to(high, (depth, CHUNK))
            parts = []
            for h in range(groups):
                here = jnp.where(high == h, 1.0, 0.0).astype(BF16)
                parts += [piece * here for piece in pieces]
            panel[...] += lax.dot_general(
                jnp.concatenate(parts, axis=0), hot, (((1,), (1,)), ((), ())),
                preferred_element_type=F32,
            )
            return carry

        lax.fori_loop(0, chunks, step, 0)
        for h in range(groups):
            own = panel[4 * depth * h : 4 * depth * (h + 1)]
            at = slice(LOW * h, LOW * (h + 1))
            spread[v, :, at] = own[0:depth] + own[depth : 2 * depth]
            wide[:, at] = own[2 * depth : 3 * depth] + own[3 * depth :]
        spread[v] = spread[v] + pltpu.roll(wide[...], 1, 1)

    def row_matrices(v):
        ids = lax.broadcasted_iota(jnp.int32, (rows, 4 * SLOT), 0).astype(F32)
        p = lanes[v]
        project = jnp.where(ids == p[0:1], p[2:3], 0.0) + jnp.where(ids == p[1:2], p[3:4], 0.0)
        ids = lax.broadcasted_iota(jnp.int32, (SLOT, rows), 1).astype(F32)
        p = columns[v]
        back = jnp.where(ids == p[:, 0:1], p[:, 4:5], 0.0)
        back = back + jnp.where(ids == p[:, 1:2], p[:, 5:6], 0.0)
        return project, back

    def by_slot(x):
        high, low = split(x)
        slot = lax.broadcasted_iota(jnp.int32, x.shape, 1) < 2 * SLOT
        return jnp.where(slot, high.astype(F32), low.astype(F32)).astype(BF16)

    def measured_along(v):
        project, back = row_matrices(v)
        mix = by_slot(jnp.dot(back, project, precision=HIGH, preferred_element_type=F32))
        back_high, back_low = split(back)
        reads[v].wait()
        data_high, data_low = split(frame[v])
        both = dot(jnp.concatenate([back_high, back_low], axis=0), data_high)
        along[v] = both[:SLOT] + both[SLOT:] + dot(back_high, data_low)
        return mix, by_slot(project)

    writes = [
        pltpu.make_async_copy(frame.at[v], residual.at[v], write_sem.at[v]) for v in range(views)
    ]

    def subtract(v, project):
        frame[v] = frame[v] - dot(project, stack[v])
        writes[v].start()

    def to_pair(v):
        core_copy(v).wait_recv()
        mine[v] = spread[v, :, my_cols] + from_core[v]
        pair_copy(v).start()

    def to_onward(v):
        pair_copy(v).wait_recv()

        @pl.when(has_onward)
        def _():
            pass_copy(v).start()

    def to_backward(v, mix):
        @pl.when(has_backward)
        def _():
            pass_copy(v).wait_recv()

        slices = jnp.concatenate(
            [from_pair[v], mine[v], from_far[v], jnp.zeros((SLOT - 3 * depth, part), F32)], axis=0
        )
        high, low = split(slices)
        stack[v, 0:SLOT] = high
        stack[v, SLOT : 2 * SLOT] = low
        stack[v, 2 * SLOT : 3 * SLOT] = high
        stack[v, 3 * SLOT :] = low
        along[v] = along[v] - dot(mix, stack[v])

        @pl.when(has_backward)
        def _():
            far_copy(v).start()

    def along_to_pair(v):
        @pl.when(has_onward)
        def _():
            far_copy(v).wait_recv()

        pair_out[v] = along[v, 0:depth] + far_in[v]
        near_copy(v).start()

    def along_to_core(v):
        near_copy(v).wait_recv()
        along_sum[v] = along[v, depth : 2 * depth] + pair_in[v]
        last_copy(v).start()

    def gather_view(v):
        last_copy(v).wait_recv()
        wide[:, my_cols] = along_sum[v]
        wide[:, other_cols] = along_core[v]
        here = wide[...]
        for t, values in enumerate((here, pltpu.roll(here, 2 * part - 1, 1))):
            for piece, x in enumerate(split(values)):
                for h in range(groups):
                    taps_left[piece, t, depth * h : depth * (h + 1)] = x[:, LOW * h : LOW * (h + 1)]

        def step(j, carry):
            at = pl.ds(pl.multiple_of(j * CHUNK, CHUNK), CHUNK)
            high, _, wa, wb = voxel_rows(v, j)
            high = jnp.broadcast_to(high, (depth, CHUNK))
            hot = low_hot[v, :, at]
            total = jnp.zeros((depth, CHUNK), F32) if v == 0 else gradient[:, at]
            for t, w in enumerate((wa, wb)):
                picked = dot(taps_left[0, t], hot) + dot(taps_left[1, t], hot)
                found = picked[:depth]
                for h in range(1, groups):
                    found = jnp.where(high == h, picked[depth * h : depth * (h + 1)], found)
                total = total + found * w
            gradient[:, at] = total * (1.0 / views) if v == views - 1 else total
            return carry

        lax.fori_loop(0, chunks, step, 0)
    mixes, projects = {}, {}

    def prepare(v):
        mixes[v], projects[v] = measured_along(v)

    def begin(v):
        spread_view(v)
        core_copy(v).start()

    steps = (
        begin,
        to_pair,
        prepare,
        to_onward,
        lambda v: to_backward(v, mixes[v]),
        along_to_pair,
        lambda v: subtract(v, projects[v]),
        along_to_core,
        gather_view,
    )
    for turn in order_of(views):
        steps[turn[0]](turn[1])

    for v in range(views):
        core_copy(v).wait_send()
        pair_copy(v).wait_send()
        near_copy(v).wait_send()
        last_copy(v).wait_send()

        @pl.when(has_onward)
        def _():
            pass_copy(v).wait_send()

        @pl.when(has_backward)
        def _():
            far_copy(v).wait_send()

        writes[v].wait()


def on_device(
    volume, measured, band_start, band_length, row_offset, row_weight, col_index, col_weight
):
    slab = lax.axis_index("slab")
    depth, cells = volume.shape
    views, rows, part = measured.shape
    taps = row_offset.shape[1]
    start = jnp.repeat(band_start, depth, axis=1)[:, None, :]
    length = jnp.repeat(band_length, depth, axis=1)[:, None, :]
    row = (start + row_offset - slab * rows).astype(F32)
    live = jnp.where(row_offset < length, row_weight, 0.0)
    rest = jnp.zeros((views, 8 - 3 * taps, row.shape[2]), F32)
    table = jnp.concatenate([row, row_weight, live, rest], axis=1)
    table = jnp.pad(table, ((0, 0), (0, 0), (depth, depth)))
    pair = slab + 1 - 2 * lax.rem(slab, 2)
    table = jnp.concatenate(
        [
            lax.dynamic_slice_in_dim(table, (at + 1) * depth, depth, 2)
            for at in (pair, slab, 2 * slab - pair)
        ],
        axis=2,
    )
    table = jnp.pad(table, ((0, 0), (0, 0), (0, SLOT - 3 * depth)))
    lanes = jnp.tile(table, (1, 1, 4))
    columns = jnp.swapaxes(table, 1, 2)

    vmem, dma = pltpu.VMEM, pltpu.SemaphoreType.DMA
    in_vmem, anywhere = pl.BlockSpec(memory_space=pltpu.VMEM), pl.BlockSpec(memory_space=pl.ANY)
    groups = 2 * part // LOW
    return pl.pallas_call(
        kernel,
        out_shape=(
            jax.ShapeDtypeStruct(measured.shape, F32),
            jax.ShapeDtypeStruct(volume.shape, F32),
        ),
        in_specs=[in_vmem] * 5 + [anywhere],
        out_specs=(anywhere, in_vmem),
        scratch_shapes=[
            vmem((views, LOW, cells), BF16),
            vmem((4 * depth * groups, LOW), F32),
            vmem((views, rows, part), F32),
            vmem((views, depth, 2 * part), F32),
            vmem((views, depth, part), F32),
            vmem((views, depth, part), F32),
            vmem((views, depth, part), F32),
            vmem((views, depth, part), F32),
            vmem((views, 4 * SLOT, part), BF16),
            vmem((depth, 2 * part), F32),
            vmem((views, SLOT, part), F32),
            vmem((views, depth, part), F32),
            vmem((views, depth, part), F32),
            vmem((views, depth, part), F32),
            vmem((views, depth, part), F32),
            vmem((views, depth, part), F32),
            vmem((2, 2, depth * groups, LOW), BF16),
        ]
        + [dma((views,))] * 14,
        compiler_params=pltpu.CompilerParams(
            collective_id=0, has_side_effects=True, vmem_limit_bytes=56 * 1024 * 1024
        ),
    )(volume, col_index, col_weight, lanes, columns, measured)


def solution(mesh):
    return jax.shard_map(
        on_device,
        mesh=mesh,
        in_specs=(P(("grp", "slab"), "blk"), P("grp", "slab", "blk"), P(), P(), P(), P(), P(), P()),
        out_specs=(P("grp", "slab", "blk"), P(("grp", "slab"), "blk")),
        check_vma=False,
    )
```

```python
import jax
import jax.numpy as jnp
from jax import lax
from jax.experimental import pallas as pl
from jax.experimental.pallas import tpu as pltpu
from jax.sharding import PartitionSpec as P

HIGH = lax.Precision.HIGHEST
F32 = jnp.float32
BF16 = jnp.bfloat16
LOW = 256
CHUNK = 1024
SLOT = 64


def split(x):
    high = x.astype(BF16)
    return high, (x - high.astype(F32)).astype(BF16)


def dot(a, b):
    return jnp.dot(a, b, preferred_element_type=F32)


ORDER = (
    ("b", 0), ("b", 1), ("p", 0), ("b", 2), ("p", 1), ("t", 0), ("o", 0), ("t", 1), ("p", 2),
    ("m", 0), ("o", 1), ("w", 0), ("t", 2), ("m", 1), ("o", 2), ("w", 1), ("a", 0), ("m", 2),
    ("w", 2), ("a", 1), ("s", 0), ("s", 1), ("c", 0), ("a", 2), ("s", 2), ("c", 1), ("g", 0),
    ("c", 2), ("g", 1), ("g", 2),
)


def kernel(
    volume, col_index, col_weight, row_offset, row_weight, band_start, band_length, measured,
    residual, gradient,
    low_hot, panel, frame, spread, from_core, mine, from_pair, from_far, stack, wide, along,
    far_in, pair_out, pair_in, along_sum, along_core, taps_left, core_send, core_recv,
    pair_send, pair_recv, pass_send, pass_recv, far_send, far_recv, near_send, near_recv,
    last_send, last_recv, read_sem, write_sem,
):
    slab, blk = lax.axis_index("slab"), lax.axis_index("blk")
    slabs = lax.axis_size("slab")
    other = 1 - blk
    depth, cells = volume.shape
    views, rows, part = measured.shape
    groups = 2 * part // LOW
    chunks = cells // CHUNK
    pair = slab + 1 - 2 * lax.rem(slab, 2)
    onward, backward = slab + 2 * (pair - slab), slab - 2 * (pair - slab)
    has_onward = jnp.logical_and(onward >= 0, onward < slabs)
    has_backward = jnp.logical_and(backward >= 0, backward < slabs)

    reads = [
        pltpu.make_async_copy(measured.at[v], frame.at[v], read_sem.at[v]) for v in range(views)
    ]
    for copy in reads:
        copy.start()
    barrier = pltpu.get_barrier_semaphore()
    pl.semaphore_signal(barrier, inc=1, device_id={"blk": other})

    pl.semaphore_signal(barrier, inc=1, device_id={"slab": pair})

    @pl.when(has_onward)
    def _():
        pl.semaphore_signal(barrier, inc=1, device_id={"slab": onward})

    @pl.when(has_backward)
    def _():
        pl.semaphore_signal(barrier, inc=1, device_id={"slab": backward})

    def await_barrier():
        pl.semaphore_wait(barrier, 2 + jnp.where(has_onward, 1, 0) + jnp.where(has_backward, 1, 0))

    def remote(source, target, send, recv, device):
        return pltpu.make_async_remote_copy(
            src_ref=source, dst_ref=target, send_sem=send, recv_sem=recv, device_id=device
        )

    def voxel_rows(v, j):
        at = pl.ds(pl.multiple_of(blk * cells + j * CHUNK, CHUNK), CHUNK)
        index, weight = col_index[v, :, at], col_weight[v, :, at]
        first, second = index[0:1], index[1:2]
        ordered = first <= second
        base = jnp.minimum(first, second)
        wa = jnp.where(ordered, weight[0:1], weight[1:2])
        wb = jnp.where(ordered, weight[1:2], weight[0:1])
        return lax.shift_right_logical(base, 8), lax.bitwise_and(base, LOW - 1), wa, wb

    my_cols = pl.ds(pl.multiple_of(blk * part, 128), part)
    other_cols = pl.ds(pl.multiple_of(other * part, 128), part)

    def core_copy(v):
        return remote(
            spread.at[v, :, other_cols], from_core.at[v], core_send.at[v], core_recv.at[v],
            {"blk": other},
        )

    def pair_copy(v):
        return remote(
            mine.at[v], from_pair.at[v], pair_send.at[v], pair_recv.at[v], {"slab": pair}
        )

    def pass_copy(v):
        return remote(
            from_pair.at[v], from_far.at[v], pass_send.at[v], pass_recv.at[v], {"slab": onward}
        )

    def far_copy(v):
        return remote(
            along.at[v, pl.ds(2 * depth, depth)], far_in.at[v], far_send.at[v], far_recv.at[v],
            {"slab": backward},
        )

    def near_copy(v):
        return remote(
            pair_out.at[v], pair_in.at[v], near_send.at[v], near_recv.at[v], {"slab": pair}
        )

    def last_copy(v):
        return remote(
            along_sum.at[v], along_core.at[v], last_send.at[v], last_recv.at[v], {"blk": other}
        )

    @pl.when(jnp.logical_not(has_backward))
    def _():
        from_far[...] = jnp.zeros_like(from_far)

    @pl.when(jnp.logical_not(has_onward))
    def _():
        far_in[...] = jnp.zeros_like(far_in)

    def spread_view(v):
        panel[...] = jnp.zeros_like(panel)

        def step(j, carry):
            at = pl.ds(pl.multiple_of(j * CHUNK, CHUNK), CHUNK)
            high, low, wa, wb = voxel_rows(v, j)
            ids = lax.broadcasted_iota(jnp.int32, (LOW, CHUNK), 0)
            hot = jnp.where(ids == low, 1.0, 0.0).astype(BF16)
            low_hot[v, :, at] = hot
            values = volume[:, at]
            pieces = split(values * wa) + split(values * wb)
            high = jnp.broadcast_to(high, (depth, CHUNK))
            parts = []
            for h in range(groups):
                here = jnp.where(high == h, 1.0, 0.0).astype(BF16)
                parts += [piece * here for piece in pieces]
            panel[...] += lax.dot_general(
                jnp.concatenate(parts, axis=0), hot, (((1,), (1,)), ((), ())),
                preferred_element_type=F32,
            )
            return carry

        lax.fori_loop(0, chunks, step, 0)
        for h in range(groups):
            own = panel[4 * depth * h : 4 * depth * (h + 1)]
            at = slice(LOW * h, LOW * (h + 1))
            spread[v, :, at] = own[0:depth] + own[depth : 2 * depth]
            wide[:, at] = own[2 * depth : 3 * depth] + own[3 * depth :]
        spread[v] = spread[v] + pltpu.roll(wide[...], 1, 1)

    def row_table(v):
        slices = row_offset.shape[2]
        raw = jnp.concatenate(
            [row_offset[v].astype(F32), row_weight[v], jnp.zeros((4, slices), F32)], axis=0
        )
        lane = lax.broadcasted_iota(jnp.int32, (8, 4 * SLOT // 2), 1)
        table = jnp.zeros((8, 4 * SLOT // 2), F32)
        start, length = jnp.zeros_like(table), jnp.zeros_like(table)
        for place, at in enumerate((pair, slab, 2 * slab - pair)):
            shift = lax.rem((place - at) * depth + 2 * slices, slices)
            here = jnp.logical_and(lane >= place * depth, lane < (place + 1) * depth)
            table = jnp.where(here, pltpu.roll(raw, shift, 1)[:, : 2 * SLOT], table)
            held = jnp.clip(at, 0, slabs - 1)
            start = jnp.where(here, (band_start[v, held] - slab * rows).astype(F32), start)
            length = jnp.where(here, band_length[v, held].astype(F32), length)
        last = jnp.where(has_backward, 3 * depth, 2 * depth)
        table = jnp.where(lane < last, table, 0.0)
        offset, weight = table[0:2], table[2:4]
        live = jnp.where(offset < length[0:2], weight, 0.0)
        row = jnp.where(lane[0:2] < last, offset + start[0:2], 0.0)
        return jnp.concatenate([row, weight, live, jnp.zeros((2, 2 * SLOT), F32)], axis=0)

    def row_matrices(v):
        table = row_table(v)
        p = table + pltpu.roll(table, SLOT, 1)
        p = jnp.concatenate([p, p], axis=1)
        ids = lax.broadcasted_iota(jnp.int32, (rows, 4 * SLOT), 0).astype(F32)
        project = jnp.where(ids == p[0:1], p[2:3], 0.0) + jnp.where(ids == p[1:2], p[3:4], 0.0)
        p = jnp.concatenate([table, jnp.zeros((2 * SLOT - 8, 2 * SLOT), F32)], axis=0).T[:SLOT]
        ids = lax.broadcasted_iota(jnp.int32, (SLOT, rows), 1).astype(F32)
        back = jnp.where(ids == p[:, 0:1], p[:, 4:5], 0.0)
        back = back + jnp.where(ids == p[:, 1:2], p[:, 5:6], 0.0)
        return project, back

    def by_slot(x):
        high, low = split(x)
        slot = lax.broadcasted_iota(jnp.int32, x.shape, 1) < 2 * SLOT
        return jnp.where(slot, high.astype(F32), low.astype(F32)).astype(BF16)

    mixes, projects, backs = {}, {}, {}

    def tables(v):
        project, back = row_matrices(v)
        mixes[v] = by_slot(jnp.dot(back, project, precision=HIGH, preferred_element_type=F32))
        projects[v], backs[v] = by_slot(project), split(back)

    def measured_along(v):
        back_high, back_low = backs[v]
        reads[v].wait()
        data_high, data_low = split(frame[v])
        both = dot(jnp.concatenate([back_high, back_low], axis=0), data_high)
        along[v] = both[:SLOT] + both[SLOT:] + dot(back_high, data_low)

    writes = [
        pltpu.make_async_copy(frame.at[v], residual.at[v], write_sem.at[v]) for v in range(views)
    ]

    def subtract(v):
        frame[v] = frame[v] - dot(projects[v], stack[v])
        writes[v].start()

    def to_pair(v):
        core_copy(v).wait_recv()
        mine[v] = spread[v, :, my_cols] + from_core[v]
        pair_copy(v).start()

    def to_onward(v):
        pair_copy(v).wait_recv()

        @pl.when(has_onward)
        def _():
            pass_copy(v).start()

    def to_backward(v):
        @pl.when(has_backward)
        def _():
            pass_copy(v).wait_recv()

        slices = jnp.concatenate(
            [from_pair[v], mine[v], from_far[v], jnp.zeros((SLOT - 3 * depth, part), F32)], axis=0
        )
        high, low = split(slices)
        stack[v, 0:SLOT] = high
        stack[v, SLOT : 2 * SLOT] = low
        stack[v, 2 * SLOT : 3 * SLOT] = high
        stack[v, 3 * SLOT :] = low
        along[v] = along[v] - dot(mixes[v], stack[v])

        @pl.when(has_backward)
        def _():
            far_copy(v).start()

    def along_to_pair(v):
        @pl.when(has_onward)
        def _():
            far_copy(v).wait_recv()

        pair_out[v] = along[v, 0:depth] + far_in[v]
        near_copy(v).start()

    def along_to_core(v):
        near_copy(v).wait_recv()
        along_sum[v] = along[v, depth : 2 * depth] + pair_in[v]
        last_copy(v).start()

    def gather_view(v):
        last_copy(v).wait_recv()
        wide[:, my_cols] = along_sum[v]
        wide[:, other_cols] = along_core[v]
        here = wide[...]
        for t, values in enumerate((here, pltpu.roll(here, 2 * part - 1, 1))):
            for piece, x in enumerate(split(values)):
                for h in range(groups):
                    taps_left[piece, t, depth * h : depth * (h + 1)] = x[:, LOW * h : LOW * (h + 1)]

        def step(j, carry):
            at = pl.ds(pl.multiple_of(j * CHUNK, CHUNK), CHUNK)
            high, _, wa, wb = voxel_rows(v, j)
            high = jnp.broadcast_to(high, (depth, CHUNK))
            hot = low_hot[v, :, at]
            total = jnp.zeros((depth, CHUNK), F32) if v == 0 else gradient[:, at]
            for t, w in enumerate((wa, wb)):
                picked = dot(taps_left[0, t], hot) + dot(taps_left[1, t], hot)
                found = picked[:depth]
                for h in range(1, groups):
                    found = jnp.where(high == h, picked[depth * h : depth * (h + 1)], found)
                total = total + found * w
            gradient[:, at] = total * (1.0 / views) if v == views - 1 else total
            return carry

        lax.fori_loop(0, chunks, step, 0)
    def begin(v):
        spread_view(v)
        if v == 0:
            await_barrier()
        core_copy(v).start()

    steps = {
        "b": begin, "p": to_pair, "t": tables, "o": to_onward, "m": measured_along,
        "w": to_backward, "a": along_to_pair, "s": subtract, "c": along_to_core, "g": gather_view,
    }
    for step, v in ORDER:
        steps[step](v)

    for v in range(views):
        core_copy(v).wait_send()
        pair_copy(v).wait_send()
        near_copy(v).wait_send()
        last_copy(v).wait_send()

        @pl.when(has_onward)
        def _():
            pass_copy(v).wait_send()

        @pl.when(has_backward)
        def _():
            far_copy(v).wait_send()

        writes[v].wait()


def on_device(
    volume, measured, band_start, band_length, row_offset, row_weight, col_index, col_weight
):
    depth, cells = volume.shape
    views, rows, part = measured.shape
    vmem, dma = pltpu.VMEM, pltpu.SemaphoreType.DMA
    in_vmem, anywhere = pl.BlockSpec(memory_space=pltpu.VMEM), pl.BlockSpec(memory_space=pl.ANY)
    groups = 2 * part // LOW
    return pl.pallas_call(
        kernel,
        out_shape=(
            jax.ShapeDtypeStruct(measured.shape, F32),
            jax.ShapeDtypeStruct(volume.shape, F32),
        ),
        in_specs=[in_vmem] * 5 + [pl.BlockSpec(memory_space=pltpu.SMEM)] * 2
        + [pl.BlockSpec(memory_space=pltpu.HBM)],
        out_specs=(anywhere, in_vmem),
        scratch_shapes=[
            vmem((views, LOW, cells), BF16),
            vmem((4 * depth * groups, LOW), F32),
            vmem((views, rows, part), F32),
            vmem((views, depth, 2 * part), F32),
            vmem((views, depth, part), F32),
            vmem((views, depth, part), F32),
            vmem((views, depth, part), F32),
            vmem((views, depth, part), F32),
            vmem((views, 4 * SLOT, part), BF16),
            vmem((depth, 2 * part), F32),
            vmem((views, SLOT, part), F32),
            vmem((views, depth, part), F32),
            vmem((views, depth, part), F32),
            vmem((views, depth, part), F32),
            vmem((views, depth, part), F32),
            vmem((views, depth, part), F32),
            vmem((2, 2, depth * groups, LOW), BF16),
        ]
        + [dma((views,))] * 14,
        compiler_params=pltpu.CompilerParams(
            collective_id=0, has_side_effects=True, vmem_limit_bytes=56 * 1024 * 1024
        ),
    )(volume, col_index, col_weight, row_offset, row_weight, band_start, band_length, measured)


def solution(mesh):
    return jax.shard_map(
        on_device,
        mesh=mesh,
        in_specs=(P(("grp", "slab"), "blk"), P("grp", "slab", "blk"), P(), P(), P(), P(), P(), P()),
        out_specs=(P("grp", "slab", "blk"), P(("grp", "slab"), "blk")),
        check_vma=False,
    )
```

```python
import jax
import jax.numpy as jnp
from jax import lax
from jax.experimental import pallas as pl
from jax.experimental.pallas import tpu as pltpu
from jax.sharding import PartitionSpec as P

HIGH = lax.Precision.HIGHEST
F32 = jnp.float32
BF16 = jnp.bfloat16
LOW = 256
CHUNK = 1024
SLOT = 64


def split(x):
    high = x.astype(BF16)
    return high, (x - high.astype(F32)).astype(BF16)


def dot(a, b):
    return jnp.dot(a, b, preferred_element_type=F32)


ORDER = (
    ("b", 0), ("b", 1), ("p", 0), ("b", 2), ("p", 1), ("t", 0), ("o", 0), ("t", 1), ("p", 2),
    ("m", 0), ("o", 1), ("w", 0), ("t", 2), ("m", 1), ("o", 2), ("w", 1), ("a", 0), ("m", 2),
    ("w", 2), ("a", 1), ("s", 0), ("s", 1), ("c", 0), ("a", 2), ("s", 2), ("c", 1), ("g", 0),
    ("c", 2), ("g", 1), ("g", 2),
)


def kernel(
    volume, col_index, col_weight, row_offset, row_weight, band_start, band_length, measured,
    residual, gradient,
    low_hot, panel, frame, spread, from_core, mine, from_pair, from_far, stack, wide, along,
    far_in, pair_out, pair_in, along_sum, along_core, taps_left, core_send, core_recv,
    pair_send, pair_recv, pass_send, pass_recv, far_send, far_recv, near_send, near_recv,
    last_send, last_recv, read_sem, write_sem,
):
    slab, blk = lax.axis_index("slab"), lax.axis_index("blk")
    slabs = lax.axis_size("slab")
    other = 1 - blk
    depth, cells = volume.shape
    views, rows, part = measured.shape
    groups = 2 * part // LOW
    chunks = cells // CHUNK
    pair = slab + 1 - 2 * lax.rem(slab, 2)
    onward, backward = slab + 2 * (pair - slab), slab - 2 * (pair - slab)
    has_onward = jnp.logical_and(onward >= 0, onward < slabs)
    has_backward = jnp.logical_and(backward >= 0, backward < slabs)

    reads = [
        pltpu.make_async_copy(measured.at[v], frame.at[v], read_sem.at[v]) for v in range(views)
    ]
    for copy in reads:
        copy.start()
    barrier = pltpu.get_barrier_semaphore()
    pl.semaphore_signal(barrier, inc=1, device_id={"blk": other})

    pl.semaphore_signal(barrier, inc=1, device_id={"slab": pair})

    @pl.when(has_onward)
    def _():
        pl.semaphore_signal(barrier, inc=1, device_id={"slab": onward})

    @pl.when(has_backward)
    def _():
        pl.semaphore_signal(barrier, inc=1, device_id={"slab": backward})

    def await_barrier():
        pl.semaphore_wait(barrier, 2 + jnp.where(has_onward, 1, 0) + jnp.where(has_backward, 1, 0))

    def remote(source, target, send, recv, device):
        return pltpu.make_async_remote_copy(
            src_ref=source, dst_ref=target, send_sem=send, recv_sem=recv, device_id=device
        )

    def voxel_rows(v, j):
        at = pl.ds(pl.multiple_of(blk * cells + j * CHUNK, CHUNK), CHUNK)
        index, weight = col_index[v, :, at], col_weight[v, :, at]
        first, second = index[0:1], index[1:2]
        ordered = first <= second
        base = jnp.minimum(first, second)
        wa = jnp.where(ordered, weight[0:1], weight[1:2])
        wb = jnp.where(ordered, weight[1:2], weight[0:1])
        return lax.shift_right_logical(base, 8), lax.bitwise_and(base, LOW - 1), wa, wb

    my_cols = pl.ds(pl.multiple_of(blk * part, 128), part)
    other_cols = pl.ds(pl.multiple_of(other * part, 128), part)

    def core_copy(v):
        return remote(
            spread.at[v, :, other_cols], from_core.at[v], core_send.at[v], core_recv.at[v],
            {"blk": other},
        )

    half = part // 2

    def cols(n):
        return pl.ds(half * n, half)

    def pair_copy(v, n):
        return remote(
            mine.at[v, :, cols(n)], from_pair.at[v, :, cols(n)], pair_send.at[v, n],
            pair_recv.at[v, n], {"slab": pair},
        )

    def pass_copy(v, n):
        return remote(
            from_pair.at[v, :, cols(n)], from_far.at[v, :, cols(n)], pass_send.at[v, n],
            pass_recv.at[v, n], {"slab": onward},
        )

    def far_copy(v, n):
        return remote(
            along.at[v, pl.ds(2 * depth, depth), cols(n)], far_in.at[v, :, cols(n)],
            far_send.at[v, n], far_recv.at[v, n], {"slab": backward},
        )

    def near_copy(v, n):
        return remote(
            pair_out.at[v, :, cols(n)], pair_in.at[v, :, cols(n)], near_send.at[v, n],
            near_recv.at[v, n], {"slab": pair},
        )

    def last_copy(v):
        return remote(
            along_sum.at[v], along_core.at[v], last_send.at[v], last_recv.at[v], {"blk": other}
        )

    @pl.when(jnp.logical_not(has_backward))
    def _():
        from_far[...] = jnp.zeros_like(from_far)

    @pl.when(jnp.logical_not(has_onward))
    def _():
        far_in[...] = jnp.zeros_like(far_in)

    def spread_view(v):
        panel[...] = jnp.zeros_like(panel)

        def step(j, carry):
            at = pl.ds(pl.multiple_of(j * CHUNK, CHUNK), CHUNK)
            high, low, wa, wb = voxel_rows(v, j)
            ids = lax.broadcasted_iota(jnp.int32, (LOW, CHUNK), 0)
            hot = jnp.where(ids == low, 1.0, 0.0).astype(BF16)
            low_hot[v, :, at] = hot
            values = volume[:, at]
            pieces = split(values * wa) + split(values * wb)
            high = jnp.broadcast_to(high, (depth, CHUNK))
            parts = []
            for h in range(groups):
                here = jnp.where(high == h, 1.0, 0.0).astype(BF16)
                parts += [piece * here for piece in pieces]
            panel[...] += lax.dot_general(
                jnp.concatenate(parts, axis=0), hot, (((1,), (1,)), ((), ())),
                preferred_element_type=F32,
            )
            return carry

        lax.fori_loop(0, chunks, step, 0)
        for h in range(groups):
            own = panel[4 * depth * h : 4 * depth * (h + 1)]
            at = slice(LOW * h, LOW * (h + 1))
            spread[v, :, at] = own[0:depth] + own[depth : 2 * depth]
            wide[:, at] = own[2 * depth : 3 * depth] + own[3 * depth :]
        spread[v] = spread[v] + pltpu.roll(wide[...], 1, 1)

    def row_table(v):
        slices = row_offset.shape[2]
        raw = jnp.concatenate(
            [row_offset[v].astype(F32), row_weight[v], jnp.zeros((4, slices), F32)], axis=0
        )
        lane = lax.broadcasted_iota(jnp.int32, (8, 4 * SLOT // 2), 1)
        table = jnp.zeros((8, 4 * SLOT // 2), F32)
        start, length = jnp.zeros_like(table), jnp.zeros_like(table)
        for place, at in enumerate((pair, slab, 2 * slab - pair)):
            shift = lax.rem((place - at) * depth + 2 * slices, slices)
            here = jnp.logical_and(lane >= place * depth, lane < (place + 1) * depth)
            table = jnp.where(here, pltpu.roll(raw, shift, 1)[:, : 2 * SLOT], table)
            held = jnp.clip(at, 0, slabs - 1)
            start = jnp.where(here, (band_start[v, held] - slab * rows).astype(F32), start)
            length = jnp.where(here, band_length[v, held].astype(F32), length)
        last = jnp.where(has_backward, 3 * depth, 2 * depth)
        table = jnp.where(lane < last, table, 0.0)
        offset, weight = table[0:2], table[2:4]
        live = jnp.where(offset < length[0:2], weight, 0.0)
        row = jnp.where(lane[0:2] < last, offset + start[0:2], 0.0)
        return jnp.concatenate([row, weight, live, jnp.zeros((2, 2 * SLOT), F32)], axis=0)

    def row_matrices(v):
        table = row_table(v)
        p = table + pltpu.roll(table, SLOT, 1)
        p = jnp.concatenate([p, p], axis=1)
        ids = lax.broadcasted_iota(jnp.int32, (rows, 4 * SLOT), 0).astype(F32)
        project = jnp.where(ids == p[0:1], p[2:3], 0.0) + jnp.where(ids == p[1:2], p[3:4], 0.0)
        p = jnp.concatenate([table, jnp.zeros((2 * SLOT - 8, 2 * SLOT), F32)], axis=0).T[:SLOT]
        ids = lax.broadcasted_iota(jnp.int32, (SLOT, rows), 1).astype(F32)
        back = jnp.where(ids == p[:, 0:1], p[:, 4:5], 0.0)
        back = back + jnp.where(ids == p[:, 1:2], p[:, 5:6], 0.0)
        return project, back

    def by_slot(x):
        high, low = split(x)
        slot = lax.broadcasted_iota(jnp.int32, x.shape, 1) < 2 * SLOT
        return jnp.where(slot, high.astype(F32), low.astype(F32)).astype(BF16)

    mixes, projects, backs = {}, {}, {}

    def tables(v):
        project, back = row_matrices(v)
        mixes[v] = by_slot(jnp.dot(back, project, precision=HIGH, preferred_element_type=F32))
        projects[v], backs[v] = by_slot(project), split(back)

    def measured_along(v):
        back_high, back_low = backs[v]
        reads[v].wait()
        data_high, data_low = split(frame[v])
        both = dot(jnp.concatenate([back_high, back_low], axis=0), data_high)
        along[v] = both[:SLOT] + both[SLOT:] + dot(back_high, data_low)

    writes = [
        pltpu.make_async_copy(frame.at[v], residual.at[v], write_sem.at[v]) for v in range(views)
    ]

    def subtract(v):
        frame[v] = frame[v] - dot(projects[v], stack[v])
        writes[v].start()

    def to_pair(v):
        core_copy(v).wait_recv()
        mine[v] = spread[v, :, my_cols] + from_core[v]
        for n in range(2):
            pair_copy(v, n).start()

    def to_onward(v):
        for n in range(2):
            pair_copy(v, n).wait_recv()

            @pl.when(has_onward)
            def _(n=n):
                pass_copy(v, n).start()

    def to_backward(v):
        for n in range(2):

            @pl.when(has_backward)
            def _(n=n):
                pass_copy(v, n).wait_recv()

            slices = jnp.concatenate(
                [
                    from_pair[v, :, cols(n)], mine[v, :, cols(n)], from_far[v, :, cols(n)],
                    jnp.zeros((SLOT - 3 * depth, half), F32),
                ],
                axis=0,
            )
            high, low = split(slices)
            for place, x in enumerate((high, low, high, low)):
                stack[v, SLOT * place : SLOT * (place + 1), cols(n)] = x
            along[v, :, cols(n)] = along[v, :, cols(n)] - dot(mixes[v], stack[v, :, cols(n)])

            @pl.when(has_backward)
            def _(n=n):
                far_copy(v, n).start()

    def along_to_pair(v):
        for n in range(2):

            @pl.when(has_onward)
            def _(n=n):
                far_copy(v, n).wait_recv()

            pair_out[v, :, cols(n)] = along[v, 0:depth, cols(n)] + far_in[v, :, cols(n)]
            near_copy(v, n).start()

    def along_to_core(v):
        for n in range(2):
            near_copy(v, n).wait_recv()
        along_sum[v] = along[v, depth : 2 * depth] + pair_in[v]
        last_copy(v).start()

    def gather_view(v):
        last_copy(v).wait_recv()
        wide[:, my_cols] = along_sum[v]
        wide[:, other_cols] = along_core[v]
        here = wide[...]
        for t, values in enumerate((here, pltpu.roll(here, 2 * part - 1, 1))):
            for piece, x in enumerate(split(values)):
                for h in range(groups):
                    taps_left[piece, t, depth * h : depth * (h + 1)] = x[:, LOW * h : LOW * (h + 1)]

        def step(j, carry):
            at = pl.ds(pl.multiple_of(j * CHUNK, CHUNK), CHUNK)
            high, _, wa, wb = voxel_rows(v, j)
            high = jnp.broadcast_to(high, (depth, CHUNK))
            hot = low_hot[v, :, at]
            total = jnp.zeros((depth, CHUNK), F32) if v == 0 else gradient[:, at]
            for t, w in enumerate((wa, wb)):
                picked = dot(taps_left[0, t], hot) + dot(taps_left[1, t], hot)
                found = picked[:depth]
                for h in range(1, groups):
                    found = jnp.where(high == h, picked[depth * h : depth * (h + 1)], found)
                total = total + found * w
            gradient[:, at] = total * (1.0 / views) if v == views - 1 else total
            return carry

        lax.fori_loop(0, chunks, step, 0)
    def begin(v):
        spread_view(v)
        if v == 0:
            await_barrier()
        core_copy(v).start()

    steps = {
        "b": begin, "p": to_pair, "t": tables, "o": to_onward, "m": measured_along,
        "w": to_backward, "a": along_to_pair, "s": subtract, "c": along_to_core, "g": gather_view,
    }
    for step, v in ORDER:
        steps[step](v)

    for v in range(views):
        core_copy(v).wait_send()
        last_copy(v).wait_send()
        for n in range(2):
            pair_copy(v, n).wait_send()
            near_copy(v, n).wait_send()

            @pl.when(has_onward)
            def _(n=n):
                pass_copy(v, n).wait_send()

            @pl.when(has_backward)
            def _(n=n):
                far_copy(v, n).wait_send()

        writes[v].wait()


def on_device(
    volume, measured, band_start, band_length, row_offset, row_weight, col_index, col_weight
):
    depth, cells = volume.shape
    views, rows, part = measured.shape
    vmem, dma = pltpu.VMEM, pltpu.SemaphoreType.DMA
    in_vmem, anywhere = pl.BlockSpec(memory_space=pltpu.VMEM), pl.BlockSpec(memory_space=pl.ANY)
    groups = 2 * part // LOW
    return pl.pallas_call(
        kernel,
        out_shape=(
            jax.ShapeDtypeStruct(measured.shape, F32),
            jax.ShapeDtypeStruct(volume.shape, F32),
        ),
        in_specs=[in_vmem] * 5 + [pl.BlockSpec(memory_space=pltpu.SMEM)] * 2
        + [pl.BlockSpec(memory_space=pltpu.HBM)],
        out_specs=(anywhere, in_vmem),
        scratch_shapes=[
            vmem((views, LOW, cells), BF16),
            vmem((4 * depth * groups, LOW), F32),
            vmem((views, rows, part), F32),
            vmem((views, depth, 2 * part), F32),
            vmem((views, depth, part), F32),
            vmem((views, depth, part), F32),
            vmem((views, depth, part), F32),
            vmem((views, depth, part), F32),
            vmem((views, 4 * SLOT, part), BF16),
            vmem((depth, 2 * part), F32),
            vmem((views, SLOT, part), F32),
            vmem((views, depth, part), F32),
            vmem((views, depth, part), F32),
            vmem((views, depth, part), F32),
            vmem((views, depth, part), F32),
            vmem((views, depth, part), F32),
            vmem((2, 2, depth * groups, LOW), BF16),
        ]
        + [dma((views,))] * 2
        + [dma((views, 2))] * 8
        + [dma((views,))] * 4,
        compiler_params=pltpu.CompilerParams(
            collective_id=0, has_side_effects=True, vmem_limit_bytes=56 * 1024 * 1024
        ),
    )(volume, col_index, col_weight, row_offset, row_weight, band_start, band_length, measured)


def solution(mesh):
    return jax.shard_map(
        on_device,
        mesh=mesh,
        in_specs=(P(("grp", "slab"), "blk"), P("grp", "slab", "blk"), P(), P(), P(), P(), P(), P()),
        out_specs=(P("grp", "slab", "blk"), P(("grp", "slab"), "blk")),
        check_vma=False,
    )
```
